256 devices in a mesh: lon: 16 (over y_hi, z), lat: 16 (over x, y_lo, core).
Axes of the slice: x: 4, y: 4 (y_hi: 2, y_lo: 2; y = y_hi * 2 + y_lo), z: 8, core: 2. Of those that a mesh axis runs over, the one named last changes fastest.
Arguments:
- queries: bfloat16 [32, 1024, 512], P('lat', 'lon'), may hold values from -32 to 32
- keys: bfloat16 [32, 1024, 512], P('lat', 'lon'), may hold values from -32 to 32
- values: bfloat16 [32, 1024, 512], P('lat', 'lon'), may hold values from -6 to 6
- upstream: bfloat16 [32, 1024, 1024], P('lat', 'lon'), may hold values from -6 to 6
- out_weight: bfloat16 [512, 1024], replicated, may hold values from -0.25 to 0.25
- average: float32 [512, 1024], P('lat'), may hold values from -6 to 6
- nbr_lon: int32 [32, 16, 8], P('lat', 'lon'), may hold values from 0 to 15, as said below
- nbr_lat: int32 [32, 16, 8], P('lat', 'lon'), may hold values from 0 to 1, as said below
- counts: int32 [32, 16], P('lat', 'lon'), may hold values from 1 to 8
Outputs:
- grad_queries: bfloat16 [32, 1024, 512], P('lat', 'lon')
- grad_keys: bfloat16 [32, 1024, 512], P('lat', 'lon')
- grad_values: bfloat16 [32, 1024, 512], P('lat', 'lon')
- updated: float32 [512, 1024], P('lat')
- next_weights: bfloat16 [512, 1024], replicated
The draws below stay inside these ranges and needn't reach their ends.
Inputs may be any that keep to these rules, and one draw needn't show every extreme that they name: `nbr_lon`: slot 0 of each list names the query's own longitude block. `nbr_lat`: rows are counted within the query's own band of 2 rows; slot 0 names the query's own row.
All inputs are finite; a program needn't handle non-finite values.
Results may differ from the reference program's by a relative error of at most 0.024.
Values may be sent and summed in bfloat16 or wider, within the bound.
No kernel may reach another device: no remote copies, remote signals or barrier semaphores. Data moves between devices by JAX's collectives and lax.ppermute only.
A program may use at most 64 MiB of HBM per device.

```python
import jax
import jax.numpy as jnp
from jax import lax

D = 1024
HEADS = 8
HEAD = 64
BLOCK = 64
NB = 8
ROWS = 2
HD = 512
LAT = 32
LONB = 16
LON = 1024
N_LAT = 16


def draw_keys(key, part):
    key = jax.random.fold_in(key, 21)
    return jnp.clip(jax.random.normal(key, (LAT, LON, HD), jnp.float32), -6.0, 6.0).astype(jnp.bfloat16)


def draw_queries(key, part):
    own_draw = jnp.clip(jax.random.normal(jax.random.fold_in(key, 31), (LAT, LON, HD), jnp.float32), -6.0, 6.0)
    return own_draw.astype(jnp.bfloat16)


def draw_nbr_lon(key, part):
    key = jax.random.fold_in(key, 11)
    picks = jax.random.randint(key, (LAT, LONB, NB), 0, LONB)
    own_block = jnp.broadcast_to(jnp.arange(LONB)[None, :, None], (LAT, LONB, NB))
    first_slot = jnp.arange(NB)[None, None, :] == 0
    return jnp.where(first_slot, own_block, picks).astype(jnp.int32)


def draw_nbr_lat(key, part):
    key = jax.random.fold_in(key, 12)
    picks = jax.random.randint(key, (LAT, LONB, NB), 0, ROWS)
    own_row = jnp.broadcast_to((jnp.arange(LAT) % ROWS)[:, None, None], (LAT, LONB, NB))
    first_slot = jnp.arange(NB)[None, None, :] == 0
    return jnp.where(first_slot, own_row, picks).astype(jnp.int32)


def plant(entries, own_key, low, top_value):
    index_at = [jax.random.randint(jax.random.fold_in(own_key, axis), (), 0, length) for axis, length in enumerate(entries.shape)]
    longest = entries.shape.index(max(entries.shape))
    beside = index_at[:longest] + [(index_at[longest] + 1) % entries.shape[longest]] + index_at[longest + 1:]
    return entries.at[tuple(index_at)].set(low).at[tuple(beside)].set(top_value)


def steps_of(key, shape, split, low, largest):
    gain, own = 1.0, jax.random.fold_in(key, 6)
    for position, shards_of in split:
        steps = jnp.exp(jax.random.uniform(jax.random.fold_in(own, position), (shards_of,), jnp.float32, low / len(split), largest / len(split)))
        gain = gain * jnp.repeat(steps, shape[position] // shards_of).reshape([-1 if axis == position else 1 for axis in range(len(shape))])
    return gain


def centred(rng, extent, scale, limit, pieces=(), held_as=jnp.bfloat16):
    factor_of = steps_of(rng, extent, pieces, -0.22, 0.18) if pieces else 1.0
    values = jax.random.normal(rng, extent, jnp.float32) * scale * factor_of
    return jnp.minimum(jnp.maximum(values, -limit), limit).astype(held_as)


def setup_inputs(seed: int = 0) -> dict:
    streams_of = jax.random.split(jax.random.key(seed), 10)
    return {
        "queries": draw_queries(jax.random.fold_in(streams_of[9], 71), 0),
        "keys": draw_keys(jax.random.fold_in(streams_of[9], 71), 0),
        "values": centred(streams_of[2], (LAT, LON, HD), 1.0, 6.0, ((0, 16), (1, 16))),
        "upstream": centred(streams_of[3], (LAT, LON, D), 1.0, 6.0, ((0, 16), (1, 16))),
        "out_weight": centred(streams_of[4], (HD, D), HD ** -0.5, 0.25),
        "average": centred(streams_of[5], (HD, D), 1.0, 6.0, ((0, 16),), jnp.float32),
        "nbr_lon": draw_nbr_lon(jax.random.fold_in(streams_of[9], 71), 0),
        "nbr_lat": draw_nbr_lat(jax.random.fold_in(streams_of[9], 71), 0),
        "counts": plant(jax.random.randint(streams_of[8], (LAT, LONB), 1, NB + 1), jax.random.fold_in(streams_of[8], 1), 1, NB).astype(jnp.int32),
    }


learn_rate = 0.01
decay_rate = 0.9
highest = lax.Precision.HIGHEST


def band_grads(items):
    query_band, key_band, value_band, grad_band, lon_list, lat_list, used_count = items
    score_scale = HEAD ** -0.5
    cells = ROWS * LON
    block_ids = lat_list * LONB + lon_list
    live_slots = jnp.arange(NB)[None, :] < used_count[:, None]
    match = (block_ids[:, :, None] == jnp.arange(ROWS * LONB)[None, None, :]) & live_slots[:, :, None]
    allowed = jnp.any(match, axis=1)
    visible = jnp.repeat(jnp.repeat(allowed, BLOCK, 0), BLOCK, 1)
    query_f = query_band.astype(jnp.float32).reshape(cells, HEADS, HEAD)
    key_f = key_band.astype(jnp.float32).reshape(cells, HEADS, HEAD)
    value_f = value_band.astype(jnp.float32).reshape(cells, HEADS, HEAD)
    grad_f = grad_band.astype(jnp.float32).reshape(cells, HEADS, HEAD)
    scores = jnp.einsum('chd,ehd->hce', query_f, key_f, precision=highest) * score_scale
    scores = jnp.where(visible[None], scores, -jnp.inf)
    highest_score = jnp.max(scores, -1, keepdims=True)
    lse = highest_score + jnp.log(jnp.sum(jnp.exp(scores - highest_score), -1, keepdims=True))
    probs = jnp.exp(scores - lse)
    attended = jnp.einsum('hce,ehd->chd', probs, value_f, precision=highest).reshape(cells, HD).astype(jnp.bfloat16)
    attended_f = attended.astype(jnp.float32).reshape(cells, HEADS, HEAD)
    delta = jnp.einsum('chd,chd->hc', grad_f, attended_f, precision=highest)
    prob_grad = jnp.einsum('chd,ehd->hce', grad_f, value_f, precision=highest)
    prob_bf = lax.optimization_barrier(probs.astype(jnp.bfloat16)).astype(jnp.float32)
    score_grad = lax.optimization_barrier((probs * (prob_grad - delta[:, :, None])).astype(jnp.bfloat16)).astype(jnp.float32)
    grad_v = jnp.einsum('hce,chd->ehd', prob_bf, grad_f, precision=highest)
    grad_q = jnp.einsum('hce,ehd->chd', score_grad, key_f, precision=highest) * score_scale
    grad_k = jnp.einsum('hce,chd->ehd', score_grad, query_f, precision=highest) * score_scale
    return (grad_q.reshape(cells, HD).astype(jnp.bfloat16), grad_k.reshape(cells, HD).astype(jnp.bfloat16),
            grad_v.reshape(cells, HD).astype(jnp.bfloat16), attended)


def reference(queries, keys, values, upstream, out_weight, average, nbr_lon, nbr_lat, counts):
    upstream_flat = upstream.reshape(LAT * LON, D)
    attn_grad = jnp.dot(upstream_flat, out_weight.T, preferred_element_type=jnp.float32).astype(jnp.bfloat16)
    bands = N_LAT
    items = (queries.reshape(bands, ROWS * LON, HD), keys.reshape(bands, ROWS * LON, HD),
             values.reshape(bands, ROWS * LON, HD), attn_grad.reshape(bands, ROWS * LON, HD),
             nbr_lon.reshape(bands, ROWS * LONB, NB), nbr_lat.reshape(bands, ROWS * LONB, NB),
             counts.reshape(bands, ROWS * LONB))
    grad_q, grad_k, grad_v, attended = lax.map(band_grads, items)
    weight_grad = jnp.dot(attended.reshape(LAT * LON, HD).T, upstream_flat, preferred_element_type=jnp.float32)
    updated = out_weight.astype(jnp.float32) - learn_rate * weight_grad
    next_weights = (decay_rate * average + (1.0 - decay_rate) * updated).astype(jnp.bfloat16)
    return (grad_q.reshape(LAT, LON, HD), grad_k.reshape(LAT, LON, HD), grad_v.reshape(LAT, LON, HD),
            updated, next_weights)
```

```python
import jax
import jax.numpy as jnp
from jax import lax
from jax.experimental import pallas as pl
from jax.experimental.pallas import tpu as pltpu
from jax.sharding import PartitionSpec as P

D = 1024
HEADS = 8
HEAD = 64
BLOCK = 64
NB = 8
ROWS = 2
HD = 512
CELLS = ROWS * BLOCK
PAIR = 2 * HEAD

learn_rate = 0.01
decay_rate = 0.9

BF = jnp.bfloat16
F32 = jnp.float32
VMEM_BYTES = 56 * 2**20


def dot(a, b, dims):
    return lax.dot_general(a, b, ((dims[:1], dims[1:]), ((), ())), preferred_element_type=F32)


def pack_kernel(q_ref, k_ref, v_ref, up_ref, w_ref, allow_ref, out_ref):
    grad = dot(up_ref[...], w_ref[...], (1, 1)).astype(BF)
    for h in range(HEADS):
        feats = slice(h * HEAD, (h + 1) * HEAD)
        kv = jnp.concatenate([k_ref[:, feats], v_ref[:, feats]], axis=1)
        qg = jnp.concatenate([q_ref[:, feats], grad[:, feats]], axis=1)
        for r in range(ROWS):
            slab = r * HEADS + h
            out_ref[slab, 0:BLOCK, :] = qg[r * BLOCK : (r + 1) * BLOCK]
            out_ref[slab, BLOCK : BLOCK + CELLS, :] = kv
            out_ref[slab, BLOCK + CELLS :, :] = allow_ref[r]


def attend_kernel(in_ref, out_ref, acc_ref, tile):
    lonb = in_ref.shape[0]
    keys = lonb * CELLS
    per = tile // BLOCK
    kv = in_ref[:, BLOCK : BLOCK + CELLS, :].reshape(keys, PAIR)
    low = lax.broadcasted_iota(jnp.int32, (1, PAIR), 1) < HEAD
    zero = jnp.zeros((), BF)
    scale = HEAD**-0.5
    k_only = jnp.where(low, kv, zero) * jnp.asarray(scale, BF)
    v_only = jnp.where(low, zero, kv)
    kv_t = kv.T
    lists = in_ref[:, BLOCK + CELLS, :].astype(F32)
    acc_ref[...] = jnp.zeros_like(acc_ref)
    for t in range(lonb // per):
        x = in_ref[t * per : (t + 1) * per, 0:BLOCK, :].reshape(tile, PAIR)
        spread = (
            lax.broadcasted_iota(jnp.int32, (lonb, tile), 0)
            == t * per + lax.broadcasted_iota(jnp.int32, (lonb, tile), 1) // BLOCK
        ).astype(F32)
        seen = dot(lists, spread, (0, 0))[: lonb * ROWS]
        bias = jnp.where(seen > 0.5, 0.0, -1e30)[:, None, :]
        scores = dot(k_only, x, (1, 1)).reshape(lonb * ROWS, BLOCK, tile) + bias
        scores = scores.reshape(keys, tile)
        top = jnp.max(scores, axis=0, keepdims=True)
        probs = jnp.exp(scores - top)
        probs = probs * (1.0 / jnp.sum(probs, axis=0, keepdims=True))
        prob_bf = probs.astype(BF)
        x_t = x.T
        att_t = dot(kv_t, prob_bf, (1, 0)).astype(BF)
        delta = jnp.sum((x_t.astype(F32) * att_t.astype(F32))[HEAD:], axis=0, keepdims=True)
        prob_grad = dot(v_only, x, (1, 1))
        score_grad = (probs * (prob_grad - delta)).astype(BF)
        grad_q_t = (dot(kv_t[:HEAD], score_grad, (1, 0)) * scale).astype(BF)
        mine = jnp.concatenate([grad_q_t, att_t[HEAD:]], axis=0).T
        out_ref[t * per : (t + 1) * per, 0:BLOCK, :] = mine.reshape(per, BLOCK, PAIR)
        acc_ref[...] += jnp.where(low, dot(score_grad, x, (1, 0)) * scale, dot(prob_bf, x, (1, 0)))
    out_ref[:, BLOCK : BLOCK + CELLS, :] = acc_ref[...].astype(BF).reshape(lonb, CELLS, PAIR)


def unpack_kernel(in_ref, up_ref, gq_ref, gk_ref, gv_ref, weight_ref):
    att = []
    for h in range(HEADS):
        feats = slice(h * HEAD, (h + 1) * HEAD)
        mine = jnp.concatenate([in_ref[r * HEADS + h, 0:BLOCK, :] for r in range(ROWS)], axis=0)
        gq_ref[:, feats] = mine[:, :HEAD]
        att.append(mine[:, HEAD:])
        kv = sum(in_ref[r * HEADS + h, BLOCK : BLOCK + CELLS, :].astype(F32) for r in range(ROWS)).astype(BF)
        gk_ref[:, feats] = kv[:, :HEAD]
        gv_ref[:, feats] = kv[:, HEAD:]
    att = jnp.concatenate(att, axis=1)
    weight_ref[...] = dot(att, up_ref[...], (0, 0)).astype(weight_ref.dtype)


def call(kernel, outs, *args, scratch=()):
    return pl.pallas_call(
        kernel,
        out_shape=outs,
        scratch_shapes=scratch,
        compiler_params=pltpu.CompilerParams(vmem_limit_bytes=VMEM_BYTES),
    )(*args)


def summed(parts, rows):
    return jnp.sum(parts.reshape(-1, rows, D).astype(F32), axis=0)


def spread(shard, axis):
    copies = jnp.broadcast_to(shard[None], (lax.axis_size(axis), *shard.shape))
    return lax.all_to_all(copies, axis, 0, 0, tiled=True).reshape(-1, D)


def on_device(queries, keys, values, upstream, out_weight, average, nbr_lon, nbr_lat, counts):
    lonb = lax.axis_size("lon")
    up = upstream.reshape(CELLS, D)
    live = jnp.arange(NB)[None, :] < counts
    block = nbr_lon.reshape(ROWS, NB) * ROWS + nbr_lat.reshape(ROWS, NB)
    allow = jnp.any(live[:, :, None] & (block[:, :, None] == jnp.arange(PAIR)[None, None, :]), axis=1)
    allow = jnp.broadcast_to(allow.astype(BF)[:, None, :], (ROWS, 16, PAIR))
    slabs = call(
        pack_kernel,
        jax.ShapeDtypeStruct((lonb, BLOCK + CELLS + 16, PAIR), BF),
        queries.reshape(CELLS, HD),
        keys.reshape(CELLS, HD),
        values.reshape(CELLS, HD),
        up,
        out_weight,
        allow,
    )
    slabs = lax.all_to_all(slabs, "lon", 0, 0, tiled=True)
    done = call(
        lambda i, o, a: attend_kernel(i, o, a, 256),
        jax.ShapeDtypeStruct((lonb, BLOCK + CELLS, PAIR), BF),
        slabs,
        scratch=[pltpu.VMEM((lonb * CELLS, PAIR), F32)],
    )
    done = lax.all_to_all(done, "lon", 0, 0, tiled=True)
    cell_grads = jax.ShapeDtypeStruct((CELLS, HD), BF)
    gq, gk, gv, weight_part = call(
        unpack_kernel,
        (cell_grads, cell_grads, cell_grads, jax.ShapeDtypeStruct((HD, D), BF)),
        done,
        up,
    )
    rows = HD // lax.axis_size("lat")
    share = rows // lonb
    band_sum = summed(lax.all_to_all(weight_part, "lat", 0, 0, tiled=True), rows).astype(BF)
    grid_sum = summed(lax.all_to_all(band_sum, "lon", 0, 0, tiled=True), share).astype(BF)
    weight_grad = spread(grid_sum, "lon").astype(F32)
    own_weight = lax.dynamic_slice_in_dim(out_weight, lax.axis_index("lat") * rows, rows, 0).astype(F32)
    updated = own_weight - learn_rate * weight_grad
    averaged = decay_rate * average + (1.0 - decay_rate) * updated
    next_weights = spread(averaged.astype(BF), "lat")
    own = (ROWS, BLOCK, HD)
    return (gq.reshape(own), gk.reshape(own), gv.reshape(own), updated, next_weights)


def solution(mesh):
    cells = P("lat", "lon", None)
    return jax.shard_map(
        on_device,
        mesh=mesh,
        in_specs=(cells, cells, cells, cells, P(), P("lat", None), cells, cells, P("lat", "lon")),
        out_specs=(cells, cells, cells, P("lat", None), P()),
        check_vma=False,
    )
```

```python
import jax
import jax.numpy as jnp
from jax import lax
from jax.experimental import pallas as pl
from jax.experimental.pallas import tpu as pltpu
from jax.sharding import PartitionSpec as P

D = 1024
HEADS = 8
HEAD = 64
BLOCK = 64
NB = 8
ROWS = 2
HD = 512
CELLS = ROWS * BLOCK
PAIR = 2 * HEAD
HALF = BLOCK // 2
LISTS = 16
TILE = 256

learn_rate = 0.01
decay_rate = 0.9

BF = jnp.bfloat16
F32 = jnp.float32
VMEM_BYTES = 56 * 2**20
SCALE = HEAD**-0.5


def dot(a, b, dims):
    return lax.dot_general(a, b, ((dims[:1], dims[1:]), ((), ())), preferred_element_type=F32)


def low_lanes():
    return lax.broadcasted_iota(jnp.int32, (1, PAIR), 1) < HEAD


def swap(x):
    return jnp.concatenate([x[:, HEAD:], x[:, :HEAD]], axis=1)


def fold(x):
    top, bottom = x[:HALF], x[HALF:]
    low = low_lanes()
    return jnp.where(low, top, swap(bottom)), jnp.where(low, swap(top), bottom)


def unfold(first, second):
    low = low_lanes()
    return jnp.concatenate([jnp.where(low, first, swap(second)), jnp.where(low, swap(first), second)], axis=0)


def pack_kernel(lon_ref, lat_ref, count_ref, q_ref, k_ref, v_ref, up_ref, w_ref, out_ref):
    grad = dot(up_ref[...], w_ref[...], (1, 1)).astype(BF)
    for h in range(HEADS):
        feats = slice(h * HEAD, (h + 1) * HEAD)
        kv = jnp.concatenate([k_ref[:, feats], v_ref[:, feats]], axis=1)
        qg = jnp.concatenate([q_ref[:, feats], grad[:, feats]], axis=1)
        for r in range(ROWS):
            slab = r * HEADS + h
            out_ref[slab, 0:BLOCK, :] = qg[r * BLOCK : (r + 1) * BLOCK]
            out_ref[slab, BLOCK : BLOCK + CELLS, :] = kv
    block = lax.broadcasted_iota(jnp.int32, (LISTS, PAIR), 1)
    for r in range(ROWS):
        seen = jnp.zeros((LISTS, PAIR), F32)
        for t in range(NB):
            named = jnp.where(t < count_ref[r, 0], lon_ref[r, 0, t] * ROWS + lat_ref[r, 0, t], -1)
            seen = jnp.where(block == named, 1.0, seen)
        for h in range(HEADS):
            out_ref[r * HEADS + h, BLOCK + CELLS :, :] = seen.astype(BF)


def forward_kernel(in_ref, att_ref, prob_ref, delta_ref):
    lonb = in_ref.shape[0]
    keys = lonb * CELLS
    per = TILE // BLOCK
    kv = in_ref[:, BLOCK : BLOCK + CELLS, :].reshape(keys, PAIR)
    k_only = jnp.where(low_lanes(), kv * jnp.asarray(SCALE, BF), jnp.zeros((), BF))
    v_t = kv.T[HEAD:]
    lists = in_ref[:, BLOCK + CELLS, :].astype(F32)
    for t in range(lonb // per):
        x = in_ref[t * per : (t + 1) * per, 0:BLOCK, :].reshape(TILE, PAIR)
        spread = (
            lax.broadcasted_iota(jnp.int32, (lonb, TILE), 0)
            == t * per + lax.broadcasted_iota(jnp.int32, (lonb, TILE), 1) // BLOCK
        ).astype(F32)
        seen = dot(lists, spread, (0, 0))[: lonb * ROWS]
        bias = jnp.where(seen > 0.5, 0.0, -1e30)[:, None, :]
        scores = dot(k_only, x, (1, 1)).reshape(lonb * ROWS, BLOCK, TILE) + bias
        scores = scores.reshape(keys, TILE)
        top = jnp.max(scores, axis=0, keepdims=True)
        probs = jnp.exp(scores - top)
        probs = (probs * (1.0 / jnp.sum(probs, axis=0, keepdims=True))).astype(BF)
        prob_ref[t] = probs
        att_t = dot(v_t, probs, (1, 0)).astype(BF)
        grad_t = x.T[HEAD:].astype(F32)
        delta_ref[t] = jnp.broadcast_to(jnp.sum(grad_t * att_t.astype(F32), axis=0, keepdims=True), (8, TILE))
        for i in range(0, per, 2):
            att_ref[t * per + i], att_ref[t * per + i + 1] = fold(att_t[:, i * BLOCK : (i + 2) * BLOCK])


def backward_kernel(in_ref, prob_ref, delta_ref, out_ref, acc_ref):
    lonb = in_ref.shape[0]
    keys = lonb * CELLS
    per = TILE // BLOCK
    kv = in_ref[:, BLOCK : BLOCK + CELLS, :].reshape(keys, PAIR)
    low = low_lanes()
    v_only = jnp.where(low, jnp.zeros((), BF), kv)
    k_t = kv.T[:HEAD]
    for t in range(lonb // per):
        x = in_ref[t * per : (t + 1) * per, 0:BLOCK, :].reshape(TILE, PAIR)
        probs = prob_ref[t]
        prob_grad = dot(v_only, x, (1, 1))
        score_grad = (probs.astype(F32) * (prob_grad - delta_ref[t, 0:1, :])).astype(BF)
        grad_q = (dot(k_t, score_grad, (1, 0)) * SCALE).astype(BF)
        for i in range(0, per, 2):
            pieces = fold(grad_q[:, i * BLOCK : (i + 2) * BLOCK])
            out_ref[t * per + i, 0:HALF, :] = pieces[0]
            out_ref[t * per + i + 1, 0:HALF, :] = pieces[1]
        part = jnp.where(low, dot(score_grad, x, (1, 0)) * SCALE, dot(probs, x, (1, 0)))
        if t == 0:
            acc_ref[...] = part
        else:
            acc_ref[...] += part
    out_ref[:, HALF:, :] = acc_ref[...].astype(BF).reshape(lonb, CELLS, PAIR)


def weight_kernel(place_ref, att_ref, up_ref, keep_ref, send_ref, att_t):
    for h in range(HEADS):
        piece = unfold(att_ref[h], att_ref[HEADS + h])
        att_t[2 * h] = piece[:HALF]
        att_t[2 * h + 1] = piece[HALF:]
    place = place_ref[0]
    for ref, core in ((send_ref, 1), (keep_ref, 0)):
        rows = [att_t[place ^ (4 * dx + 2 * dy + core)] for dy in range(2) for dx in range(HEADS // 2)]
        part = dot(jnp.concatenate(rows, axis=0), up_ref[...], (1, 0))
        ref[...] = part.astype(BF).reshape(ref.shape)


def unpack_kernel(in_ref, gq_ref, gk_ref, gv_ref):
    gq_t = []
    for h in range(HEADS):
        feats = slice(h * HEAD, (h + 1) * HEAD)
        gq_t.append(unfold(in_ref[h, 0:HALF, :], in_ref[HEADS + h, 0:HALF, :]))
        kv = sum(in_ref[r * HEADS + h, HALF:, :].astype(F32) for r in range(ROWS)).astype(BF)
        gk_ref[:, feats] = kv[:, :HEAD]
        gv_ref[:, feats] = kv[:, HEAD:]
    gq_ref[...] = jnp.concatenate(gq_t, axis=0).T


def call(kernel, outs, *args, scratch=(), scalars=0):
    on_chip = [pl.BlockSpec(memory_space=pltpu.SMEM if i < scalars else pltpu.VMEM) for i in range(len(args))]
    return pl.pallas_call(
        kernel,
        out_shape=outs,
        in_specs=on_chip,
        scratch_shapes=scratch,
        compiler_params=pltpu.CompilerParams(vmem_limit_bytes=VMEM_BYTES),
    )(*args)


def shape(*dims, dtype=BF):
    return jax.ShapeDtypeStruct(dims, dtype)


def pairwise(x, axis, bit):
    return lax.ppermute(x, axis, [(i, i ^ bit) for i in range(lax.axis_size(axis))])


def plus(*parts):
    total = parts[0].astype(F32)
    for part in parts[1:]:
        total = total + part.astype(F32)
    return total


def quad_sum(x, a, b):
    x = x.astype(BF)
    return plus(x, pairwise(x, "lon", a)) + plus(pairwise(x, "lon", b), pairwise(x, "lon", a ^ b))


def on_device(queries, keys, values, upstream, out_weight, average, nbr_lon, nbr_lat, counts):
    lonb = lax.axis_size("lon")
    lats = lax.axis_size("lat")
    same_core = [[c + 2 * i for i in range(lats // 2)] for c in range(2)]
    up = upstream.reshape(CELLS, D)
    slabs = call(
        pack_kernel,
        shape(lonb, BLOCK + CELLS + LISTS, PAIR),
        nbr_lon,
        nbr_lat,
        counts,
        queries.reshape(CELLS, HD),
        keys.reshape(CELLS, HD),
        values.reshape(CELLS, HD),
        up,
        out_weight,
        scalars=3,
    )
    slabs = lax.all_to_all(slabs, "lon", 0, 0, tiled=True)
    tiles = lonb * BLOCK // TILE
    att, probs, delta = call(
        forward_kernel,
        (
            shape(lonb, HALF, PAIR),
            shape(tiles, lonb * CELLS, TILE),
            shape(tiles, 8, TILE, dtype=F32),
        ),
        slabs,
    )
    att = lax.all_to_all(att, "lon", 0, 0, tiled=True)
    grads = call(
        backward_kernel,
        shape(lonb, HALF + CELLS, PAIR),
        slabs,
        probs,
        delta,
        scratch=[pltpu.VMEM((lonb * CELLS, PAIR), F32)],
    )
    att, grads = lax.optimization_barrier((att, grads))
    rows = HD // lats
    half = shape(2, lats // 4, rows, D)
    place = lax.axis_index("lat")
    keep, send = call(
        weight_kernel,
        (half, half),
        place.reshape(1),
        att,
        up,
        scratch=[pltpu.VMEM((2 * HEADS, HALF, CELLS), BF)],
        scalars=1,
    )
    grads = lax.all_to_all(grads, "lon", 0, 0, tiled=True)
    came = pairwise(send, "lat", 1)
    by_y = pairwise(plus(keep[1], came[1]).astype(BF), "lat", 2)
    by_x = [plus(keep[0, i], came[0, i], by_y[i]) for i in range(lats // 4)]
    by_x = by_x[:1] + [pairwise(by_x[i].astype(BF), "lat", 4 * i) for i in range(1, lats // 4)]
    total = quad_sum(plus(*by_x), 1, 8)
    total = quad_sum(total, 2, 4)
    own_weight = lax.dynamic_slice_in_dim(out_weight, place * rows, rows, 0).astype(F32)
    updated = own_weight - learn_rate * total
    averaged = decay_rate * average + (1.0 - decay_rate) * updated
    averaged, grads = lax.optimization_barrier((averaged, grads))
    copies = jnp.broadcast_to(averaged.astype(BF)[None], (lats // 2, rows, D))
    mine = lax.all_to_all(copies, "lat", 0, 0, axis_index_groups=same_core, tiled=True)
    other = pairwise(mine, "lat", 1)
    first = place % 2 == 0
    next_weights = jnp.stack([jnp.where(first, mine, other), jnp.where(first, other, mine)], axis=1).reshape(HD, D)
    cell_grads = shape(CELLS, HD)
    gq, gk, gv = call(unpack_kernel, (cell_grads, cell_grads, cell_grads), grads)
    own = (ROWS, BLOCK, HD)
    return (gq.reshape(own), gk.reshape(own), gv.reshape(own), updated, next_weights)


def solution(mesh):
    cells = P("lat", "lon", None)
    return jax.shard_map(
        on_device,
        mesh=mesh,
        in_specs=(cells, cells, cells, cells, P(), P("lat", None), cells, cells, P("lat", "lon")),
        out_specs=(cells, cells, cells, P("lat", None), P()),
        check_vma=False,
    )
```

```python
import jax
import jax.numpy as jnp
from jax import lax
from jax.experimental import pallas as pl
from jax.experimental.pallas import tpu as pltpu
from jax.sharding import PartitionSpec as P

D = 1024
HEADS = 8
HEAD = 64
BLOCK = 64
NB = 8
ROWS = 2
HD = 512
CELLS = ROWS * BLOCK
PAIR = 2 * HEAD
HALF = BLOCK // 2
LISTS = 16
GROUP = 512

learn_rate = 0.01
decay_rate = 0.9

BF = jnp.bfloat16
F32 = jnp.float32
VMEM_BYTES = 56 * 2**20
SMALL_BYTES = 24 * 2**20
SCALE = HEAD**-0.5


def dot(a, b, dims):
    return lax.dot_general(a, b, ((dims[:1], dims[1:]), ((), ())), preferred_element_type=F32)


def low_lanes():
    return lax.broadcasted_iota(jnp.int32, (1, PAIR), 1) < HEAD


def swap(x):
    return jnp.concatenate([x[:, HEAD:], x[:, :HEAD]], axis=1)


def fold(x):
    top, bottom = x[:HALF], x[HALF:]
    low = low_lanes()
    return jnp.where(low, top, swap(bottom)), jnp.where(low, swap(top), bottom)


def unfold(first, second):
    low = low_lanes()
    return jnp.concatenate([jnp.where(low, first, swap(second)), jnp.where(low, swap(first), second)], axis=0)


def pack_kernel(lon_ref, lat_ref, count_ref, q_ref, k_ref, v_ref, up_ref, w_ref, out_ref):
    grad = dot(up_ref[...], w_ref[...], (1, 1)).astype(BF)
    for h in range(HEADS):
        feats = slice(h * HEAD, (h + 1) * HEAD)
        kv = jnp.concatenate([k_ref[:, feats], v_ref[:, feats]], axis=1)
        qg = jnp.concatenate([q_ref[:, feats], grad[:, feats]], axis=1)
        for r in range(ROWS):
            slab = r * HEADS + h
            out_ref[slab, 0:BLOCK, :] = qg[r * BLOCK : (r + 1) * BLOCK]
            out_ref[slab, BLOCK : BLOCK + CELLS, :] = kv
    block = lax.broadcasted_iota(jnp.int32, (LISTS, PAIR), 1)
    for r in range(ROWS):
        seen = jnp.zeros((LISTS, PAIR), F32)
        for t in range(NB):
            named = jnp.where(t < count_ref[r], lon_ref[r, 0, t] * ROWS + lat_ref[r, 0, t], -1)
            seen = jnp.where(block == named, 1.0, seen)
        for h in range(HEADS):
            out_ref[r * HEADS + h, BLOCK + CELLS :, :] = seen.astype(BF)


def seen_blocks(in_ref):
    lonb = in_ref.shape[0]
    tile = (lonb, lonb * BLOCK)
    spread = lax.broadcasted_iota(jnp.int32, tile, 0) == lax.broadcasted_iota(jnp.int32, tile, 1) // BLOCK
    return dot(in_ref[:, BLOCK + CELLS, :].astype(F32), spread.astype(F32), (0, 0))[: lonb * ROWS] > 0.5


def tiles_of(in_ref):
    lonb = in_ref.shape[0]
    x = in_ref[:, 0:BLOCK, :].reshape(lonb * BLOCK, PAIR)
    return x, in_ref[:, BLOCK : BLOCK + CELLS, :].reshape(lonb * CELLS, PAIR)


def forward_kernel(in_ref, att_ref, stat_ref, score_ref):
    x, kv = tiles_of(in_ref)
    keys, cells = score_ref.shape
    k_only = jnp.where(low_lanes(), kv * jnp.asarray(SCALE, BF), jnp.zeros((), BF))
    v_t = kv.T[HEAD:]
    seen = seen_blocks(in_ref)
    tops = []
    for g in range(0, keys, GROUP):
        scores = dot(k_only[g : g + GROUP], x, (1, 1))
        score_ref[g : g + GROUP, :] = scores
        tops += [jnp.max(scores[j : j + BLOCK], axis=0, keepdims=True) for j in range(0, GROUP, BLOCK)]
    top = jnp.max(jnp.where(seen, jnp.concatenate(tops, axis=0), -1e30), axis=0, keepdims=True)
    shift = jnp.where(seen, top, 1e30)
    att = jnp.zeros((HEAD, cells), F32)
    total = jnp.zeros((8, cells), F32)
    for g in range(0, keys, GROUP):
        probs = []
        for j in range(g, g + GROUP, BLOCK):
            prob = jnp.exp(score_ref[j : j + BLOCK, :] - shift[j // BLOCK : j // BLOCK + 1])
            total = total + jnp.sum(prob.reshape(BLOCK // 8, 8, cells), axis=0)
            probs.append(prob.astype(BF))
        att = att + dot(v_t[:, g : g + GROUP], jnp.concatenate(probs, axis=0), (1, 0))
    total = jnp.sum(total, axis=0, keepdims=True)
    att = (att * (1.0 / total)).astype(BF)
    delta = jnp.sum(x.T[HEAD:].astype(F32) * att.astype(F32), axis=0, keepdims=True)
    row = lax.broadcasted_iota(jnp.int32, stat_ref.shape, 0)
    stat_ref[...] = jnp.where(row == 0, top + jnp.log(total), delta)
    for i in range(0, cells, PAIR):
        b = i // BLOCK
        att_ref[b], att_ref[b + 1] = fold(att[:, i : i + PAIR])


def backward_kernel(in_ref, stat_ref, out_ref):
    x, kv = tiles_of(in_ref)
    keys, cells = kv.shape[0], x.shape[0]
    low = low_lanes()
    zero = jnp.zeros((), BF)
    k_only = jnp.where(low, kv * jnp.asarray(SCALE, BF), zero)
    v_only = jnp.where(low, zero, kv)
    k_t = kv.T[:HEAD]
    shift = jnp.where(seen_blocks(in_ref), stat_ref[0:1, :], 1e30)
    delta = stat_ref[1:2, :]
    grad_q = jnp.zeros((HEAD, cells), F32)
    for g in range(0, keys, GROUP):
        scores = dot(k_only[g : g + GROUP], x, (1, 1))
        prob_grad = dot(v_only[g : g + GROUP], x, (1, 1))
        probs, score_grads = [], []
        for j in range(0, GROUP, BLOCK):
            b = (g + j) // BLOCK
            prob = jnp.exp(scores[j : j + BLOCK] - shift[b : b + 1])
            probs.append(prob.astype(BF))
            score_grads.append((prob * (prob_grad[j : j + BLOCK] - delta)).astype(BF))
        probs = jnp.concatenate(probs, axis=0)
        score_grads = jnp.concatenate(score_grads, axis=0)
        grad_q = grad_q + dot(k_t[:, g : g + GROUP], score_grads, (1, 0))
        grad_kv = jnp.where(low, dot(score_grads, x, (1, 0)) * SCALE, dot(probs, x, (1, 0)))
        out_ref[g // CELLS : (g + GROUP) // CELLS, HALF:, :] = grad_kv.astype(BF).reshape(GROUP // CELLS, CELLS, PAIR)
    grad_q = (grad_q * SCALE).astype(BF)
    for i in range(0, cells, PAIR):
        b = i // BLOCK
        out_ref[b, 0:HALF, :], out_ref[b + 1, 0:HALF, :] = fold(grad_q[:, i : i + PAIR])


def weight_kernel(place_ref, att_ref, up_ref, out_ref, att_t):
    for h in range(HEADS):
        piece = unfold(att_ref[h], att_ref[HEADS + h])
        att_t[2 * h] = piece[:HALF]
        att_t[2 * h + 1] = piece[HALF:]
    place = place_ref[0]
    rows = [att_t[place ^ (4 * dx + 2 * dy)] for dy in range(2) for dx in range(HEADS // 2)]
    part = dot(jnp.concatenate(rows, axis=0), up_ref[...], (1, 0))
    out_ref[...] = part.astype(BF).reshape(out_ref.shape)


def unpack_kernel(in_ref, gq_ref, gk_ref, gv_ref):
    gq_t = []
    for h in range(HEADS):
        feats = slice(h * HEAD, (h + 1) * HEAD)
        gq_t.append(unfold(in_ref[h, 0:HALF, :], in_ref[HEADS + h, 0:HALF, :]))
        kv = sum(in_ref[r * HEADS + h, HALF:, :].astype(F32) for r in range(ROWS)).astype(BF)
        gk_ref[:, feats] = kv[:, :HEAD]
        gv_ref[:, feats] = kv[:, HEAD:]
    gq_ref[...] = jnp.concatenate(gq_t, axis=0).T


def call(kernel, outs, *args, scratch=(), scalars=0, vmem=VMEM_BYTES):
    on_chip = [pl.BlockSpec(memory_space=pltpu.SMEM if i < scalars else pltpu.VMEM) for i in range(len(args))]
    return pl.pallas_call(
        kernel,
        out_shape=outs,
        in_specs=on_chip,
        scratch_shapes=scratch,
        compiler_params=pltpu.CompilerParams(vmem_limit_bytes=vmem),
    )(*args)


def shape(*dims, dtype=BF):
    return jax.ShapeDtypeStruct(dims, dtype)


def pairwise(x, axis, bit):
    return lax.ppermute(x, axis, [(i, i ^ bit) for i in range(lax.axis_size(axis))])


def plus(*parts):
    total = parts[0].astype(F32)
    for part in parts[1:]:
        total = total + part.astype(F32)
    return total


def quad_sum(x, a, b):
    x = x.astype(BF)
    return plus(x, pairwise(x, "lon", a)) + plus(pairwise(x, "lon", b), pairwise(x, "lon", a ^ b))


def on_device(queries, keys, values, upstream, out_weight, average, nbr_lon, nbr_lat, counts):
    lonb = lax.axis_size("lon")
    lats = lax.axis_size("lat")
    same_core = [[c + 2 * i for i in range(lats // 2)] for c in range(2)]
    up = upstream.reshape(CELLS, D)
    slabs = call(
        pack_kernel,
        shape(lonb, BLOCK + CELLS + LISTS, PAIR),
        nbr_lon,
        nbr_lat,
        counts.reshape(ROWS),
        queries.reshape(CELLS, HD),
        keys.reshape(CELLS, HD),
        values.reshape(CELLS, HD),
        up,
        out_weight,
        scalars=3,
    )
    slabs = lax.all_to_all(slabs, "lon", 0, 0, tiled=True)
    cells = lonb * BLOCK
    att, stats = call(
        forward_kernel,
        (shape(lonb, HALF, PAIR), shape(8, cells, dtype=F32)),
        slabs,
        scratch=[pltpu.VMEM((lonb * CELLS, cells), F32)],
    )
    att = lax.all_to_all(att, "lon", 0, 0, tiled=True)
    grads = call(backward_kernel, shape(lonb, HALF + CELLS, PAIR), slabs, stats)
    att, grads = lax.optimization_barrier((att, grads))
    rows = HD // lats
    half = shape(2, lats // 4, rows, D)
    place = lax.axis_index("lat")
    send, keep = (
        call(
            weight_kernel,
            half,
            (place ^ core).reshape(1),
            att,
            up,
            scratch=[pltpu.VMEM((2 * HEADS, HALF, CELLS), BF)],
            scalars=1,
            vmem=SMALL_BYTES,
        )
        for core in (1, 0)
    )
    grads = lax.all_to_all(grads, "lon", 0, 0, tiled=True)
    came = pairwise(send, "lat", 1)
    by_y = pairwise(plus(keep[1], came[1]).astype(BF), "lat", 2)
    by_x = [plus(keep[0, i], came[0, i], by_y[i]) for i in range(lats // 4)]
    by_x = by_x[:1] + [pairwise(by_x[i].astype(BF), "lat", 4 * i) for i in range(1, lats // 4)]
    total = quad_sum(plus(*by_x), 1, 8)
    total = quad_sum(total, 2, 4)
    own_weight = lax.dynamic_slice_in_dim(out_weight, place * rows, rows, 0).astype(F32)
    updated = own_weight - learn_rate * total
    averaged = decay_rate * average + (1.0 - decay_rate) * updated
    cell_grads = shape(CELLS, HD)
    gq, gk, gv = call(unpack_kernel, (cell_grads, cell_grads, cell_grads), grads, vmem=SMALL_BYTES)
    averaged, gq, gk, gv = lax.optimization_barrier((averaged, gq, gk, gv))
    copies = jnp.broadcast_to(averaged.astype(BF)[None], (lats // 2, rows, D))
    mine = lax.all_to_all(copies, "lat", 0, 0, axis_index_groups=same_core, tiled=True)
    other = pairwise(mine, "lat", 1)
    first = place % 2 == 0
    next_weights = jnp.stack([jnp.where(first, mine, other), jnp.where(first, other, mine)], axis=1).reshape(HD, D)
    own = (ROWS, BLOCK, HD)
    return (gq.reshape(own), gk.reshape(own), gv.reshape(own), updated, next_weights)


def solution(mesh):
    cells = P("lat", "lon", None)
    return jax.shard_map(
        on_device,
        mesh=mesh,
        in_specs=(cells, cells, cells, cells, P(), P("lat", None), cells, cells, P("lat", "lon")),
        out_specs=(cells, cells, cells, P("lat", None), P()),
        check_vma=False,
    )
```

```python
import jax
import jax.numpy as jnp
from jax import lax
from jax.experimental import pallas as pl
from jax.experimental.pallas import tpu as pltpu
from jax.sharding import PartitionSpec as P

D = 1024
HEADS = 8
HEAD = 64
BLOCK = 64
NB = 8
ROWS = 2
HD = 512
CELLS = ROWS * BLOCK
PAIR = 2 * HEAD
HALF = BLOCK // 2
LISTS = 16
GROUP = 512

learn_rate = 0.01
decay_rate = 0.9

BF = jnp.bfloat16
F32 = jnp.float32
VMEM_BYTES = 56 * 2**20
SMALL_BYTES = 24 * 2**20
SCALE = HEAD**-0.5


def dot(a, b, dims):
    return lax.dot_general(a, b, ((dims[:1], dims[1:]), ((), ())), preferred_element_type=F32)


def low_lanes():
    return lax.broadcasted_iota(jnp.int32, (1, PAIR), 1) < HEAD


def swap(x):
    return jnp.concatenate([x[:, HEAD:], x[:, :HEAD]], axis=1)


def fold(x):
    top, bottom = x[:HALF], x[HALF:]
    low = low_lanes()
    return jnp.where(low, top, swap(bottom)), jnp.where(low, swap(top), bottom)


def unfold(first, second):
    low = low_lanes()
    return jnp.concatenate([jnp.where(low, first, swap(second)), jnp.where(low, swap(first), second)], axis=0)


def pack_kernel(lon_ref, lat_ref, count_ref, q_ref, k_ref, v_ref, up_ref, w_ref, out_ref):
    grad = dot(up_ref[...], w_ref[...], (1, 1)).astype(BF)
    for h in range(HEADS):
        feats = slice(h * HEAD, (h + 1) * HEAD)
        kv = jnp.concatenate([k_ref[:, feats], v_ref[:, feats]], axis=1)
        qg = jnp.concatenate([q_ref[:, feats], grad[:, feats]], axis=1)
        for r in range(ROWS):
            slab = r * HEADS + h
            out_ref[slab, 0:BLOCK, :] = qg[r * BLOCK : (r + 1) * BLOCK]
            out_ref[slab, BLOCK : BLOCK + CELLS, :] = kv
    block = lax.broadcasted_iota(jnp.int32, (LISTS, PAIR), 1)
    for r in range(ROWS):
        seen = jnp.zeros((LISTS, PAIR), F32)
        for t in range(NB):
            named = jnp.where(t < count_ref[r], lon_ref[r, 0, t] * ROWS + lat_ref[r, 0, t], -1)
            seen = jnp.where(block == named, 1.0, seen)
        for h in range(HEADS):
            out_ref[r * HEADS + h, BLOCK + CELLS :, :] = seen.astype(BF)


def seen_blocks(in_ref):
    lonb = in_ref.shape[0]
    tile = (lonb, lonb * BLOCK)
    spread = lax.broadcasted_iota(jnp.int32, tile, 0) == lax.broadcasted_iota(jnp.int32, tile, 1) // BLOCK
    return dot(in_ref[:, BLOCK + CELLS, :].astype(F32), spread.astype(F32), (0, 0))[: lonb * ROWS] > 0.5


def tiles_of(in_ref):
    lonb = in_ref.shape[0]
    x = in_ref[:, 0:BLOCK, :].reshape(lonb * BLOCK, PAIR)
    return x, in_ref[:, BLOCK : BLOCK + CELLS, :].reshape(lonb * CELLS, PAIR)


def forward_kernel(in_ref, att_ref, stat_ref, score_ref):
    x, kv = tiles_of(in_ref)
    keys, cells = score_ref.shape
    k_only = jnp.where(low_lanes(), kv * jnp.asarray(SCALE, BF), jnp.zeros((), BF))
    v_t = kv.T[HEAD:]
    seen = seen_blocks(in_ref)
    tops = []
    for g in range(0, keys, GROUP):
        scores = dot(k_only[g : g + GROUP], x, (1, 1))
        score_ref[g : g + GROUP, :] = scores
        tops += [jnp.max(scores[j : j + BLOCK], axis=0, keepdims=True) for j in range(0, GROUP, BLOCK)]
    top = jnp.max(jnp.where(seen, jnp.concatenate(tops, axis=0), -1e30), axis=0, keepdims=True)
    shift = jnp.where(seen, top, 1e30)
    att = jnp.zeros((HEAD, cells), F32)
    total = jnp.zeros((8, cells), F32)
    for g in range(0, keys, GROUP):
        probs = []
        for j in range(g, g + GROUP, BLOCK):
            prob = jnp.exp(score_ref[j : j + BLOCK, :] - shift[j // BLOCK : j // BLOCK + 1])
            total = total + jnp.sum(prob.reshape(BLOCK // 8, 8, cells), axis=0)
            probs.append(prob.astype(BF))
        att = att + dot(v_t[:, g : g + GROUP], jnp.concatenate(probs, axis=0), (1, 0))
    total = jnp.sum(total, axis=0, keepdims=True)
    att = (att * (1.0 / total)).astype(BF)
    delta = jnp.sum(x.T[HEAD:].astype(F32) * att.astype(F32), axis=0, keepdims=True)
    row = lax.broadcasted_iota(jnp.int32, stat_ref.shape, 0)
    stat_ref[...] = jnp.where(row == 0, top + jnp.log(total), delta)
    for i in range(0, cells, PAIR):
        b = i // BLOCK
        att_ref[b], att_ref[b + 1] = fold(att[:, i : i + PAIR])


def backward_kernel(in_ref, stat_ref, out_ref):
    x, kv = tiles_of(in_ref)
    keys, cells = kv.shape[0], x.shape[0]
    low = low_lanes()
    zero = jnp.zeros((), BF)
    k_only = jnp.where(low, kv * jnp.asarray(SCALE, BF), zero)
    v_only = jnp.where(low, zero, kv)
    k_t = kv.T[:HEAD]
    shift = jnp.where(seen_blocks(in_ref), stat_ref[0:1, :], 1e30)
    delta = stat_ref[1:2, :]
    grad_q = jnp.zeros((HEAD, cells), F32)
    for g in range(0, keys, GROUP):
        scores = dot(k_only[g : g + GROUP], x, (1, 1))
        prob_grad = dot(v_only[g : g + GROUP], x, (1, 1))
        probs, score_grads = [], []
        for j in range(0, GROUP, BLOCK):
            b = (g + j) // BLOCK
            prob = jnp.exp(scores[j : j + BLOCK] - shift[b : b + 1])
            probs.append(prob.astype(BF))
            score_grads.append((prob * (prob_grad[j : j + BLOCK] - delta)).astype(BF))
        probs = jnp.concatenate(probs, axis=0)
        score_grads = jnp.concatenate(score_grads, axis=0)
        grad_q = grad_q + dot(k_t[:, g : g + GROUP], score_grads, (1, 0))
        grad_kv = jnp.where(low, dot(score_grads, x, (1, 0)) * SCALE, dot(probs, x, (1, 0)))
        out_ref[g // CELLS : (g + GROUP) // CELLS, HALF:, :] = grad_kv.astype(BF).reshape(GROUP // CELLS, CELLS, PAIR)
    grad_q = (grad_q * SCALE).astype(BF)
    for i in range(0, cells, PAIR):
        b = i // BLOCK
        out_ref[b, 0:HALF, :], out_ref[b + 1, 0:HALF, :] = fold(grad_q[:, i : i + PAIR])


def weight_kernel(place_ref, att_ref, other_att_ref, up_ref, other_up_ref, *refs):
    *out_refs, att_t = refs
    for h in range(HEADS):
        mine = unfold(att_ref[h], att_ref[HEADS + h])
        other = unfold(other_att_ref[h], other_att_ref[HEADS + h])
        for half in range(2):
            rows = slice(half * HALF, (half + 1) * HALF)
            att_t[2 * h + half] = jnp.concatenate([mine[rows], other[rows]], axis=1)
    place = place_ref[0]
    up = jnp.concatenate([up_ref[...], other_up_ref[...]], axis=0)
    for dx, out_ref in enumerate(out_refs):
        rows = jnp.concatenate([att_t[place ^ (4 * dx + 2 * dy)] for dy in range(2)], axis=0)
        out_ref[...] = dot(rows, up, (1, 0)).astype(BF).reshape(out_ref.shape)


def unpack_kernel(in_ref, gq_ref, gk_ref, gv_ref):
    gq_t = []
    for h in range(HEADS):
        feats = slice(h * HEAD, (h + 1) * HEAD)
        gq_t.append(unfold(in_ref[h, 0:HALF, :], in_ref[HEADS + h, 0:HALF, :]))
        kv = sum(in_ref[r * HEADS + h, HALF:, :].astype(F32) for r in range(ROWS)).astype(BF)
        gk_ref[:, feats] = kv[:, :HEAD]
        gv_ref[:, feats] = kv[:, HEAD:]
    gq_ref[...] = jnp.concatenate(gq_t, axis=0).T


def call(kernel, outs, *args, scratch=(), scalars=0, vmem=VMEM_BYTES):
    on_chip = [pl.BlockSpec(memory_space=pltpu.SMEM if i < scalars else pltpu.VMEM) for i in range(len(args))]
    return pl.pallas_call(
        kernel,
        out_shape=outs,
        in_specs=on_chip,
        scratch_shapes=scratch,
        compiler_params=pltpu.CompilerParams(vmem_limit_bytes=vmem),
    )(*args)


def shape(*dims, dtype=BF):
    return jax.ShapeDtypeStruct(dims, dtype)


def pairwise(x, axis, bit):
    return lax.ppermute(x, axis, [(i, i ^ bit) for i in range(lax.axis_size(axis))])


def plus(*parts):
    total = parts[0].astype(F32)
    for part in parts[1:]:
        total = total + part.astype(F32)
    return total


def joined(x, *bits):
    x = x.astype(BF)
    one, two, three = (pairwise(x, "lon", bit) for bit in bits)
    return plus(x, one) + plus(two, three)


def paired(x, bit):
    x = x.astype(BF)
    return plus(x, pairwise(x, "lon", bit))


def on_device(queries, keys, values, upstream, out_weight, average, nbr_lon, nbr_lat, counts):
    lonb = lax.axis_size("lon")
    lats = lax.axis_size("lat")
    same_core = [[c + 2 * i for i in range(lats // 2)] for c in range(2)]
    up = upstream.reshape(CELLS, D)
    other_up = pairwise(up, "lat", 1)
    slabs = call(
        pack_kernel,
        shape(lonb, BLOCK + CELLS + LISTS, PAIR),
        nbr_lon,
        nbr_lat,
        counts.reshape(ROWS),
        queries.reshape(CELLS, HD),
        keys.reshape(CELLS, HD),
        values.reshape(CELLS, HD),
        up,
        out_weight,
        scalars=3,
    )
    slabs = lax.all_to_all(slabs, "lon", 0, 0, tiled=True)
    cells = lonb * BLOCK
    att, stats = call(
        forward_kernel,
        (shape(lonb, HALF, PAIR), shape(8, cells, dtype=F32)),
        slabs,
        scratch=[pltpu.VMEM((lonb * CELLS, cells), F32)],
    )
    att = lax.all_to_all(att, "lon", 0, 0, tiled=True)
    grads = call(backward_kernel, shape(lonb, HALF + CELLS, PAIR), slabs, stats)
    att, grads = lax.optimization_barrier((att, grads))
    rows = HD // lats
    quarters = lats // 4
    place = lax.axis_index("lat")
    parts = call(
        weight_kernel,
        [shape(2, rows, D)] * quarters,
        place.reshape(1),
        att,
        pairwise(att, "lat", 1),
        up,
        other_up,
        scratch=[pltpu.VMEM((2 * HEADS, HALF, 2 * CELLS), BF)],
        scalars=1,
        vmem=SMALL_BYTES,
    )
    grads = lax.all_to_all(grads, "lon", 0, 0, tiled=True)
    parts = [parts[0]] + [pairwise(parts[i], "lat", 4 * i) for i in range(1, quarters)]
    near, far = (plus(*(part[i] for part in parts)).astype(BF) for i in range(2))
    both = [(i, j) for i in range(lonb) for j in range(lats)]
    across = lax.ppermute(far, ("lon", "lat"), [(i * lats + j, (i ^ 8) * lats + (j ^ 2)) for i, j in both])
    total = plus(near, pairwise(near, "lon", 8)) + plus(pairwise(far, "lat", 2), across)
    total = paired(joined(total, 1, 2, 3), 6)
    own_weight = lax.dynamic_slice_in_dim(out_weight, place * rows, rows, 0).astype(F32)
    updated = own_weight - learn_rate * total
    averaged = decay_rate * average + (1.0 - decay_rate) * updated
    averaged, grads = lax.optimization_barrier((averaged, grads))
    copies = jnp.broadcast_to(averaged.astype(BF)[None], (lats // 2, rows, D))
    mine = lax.all_to_all(copies, "lat", 0, 0, axis_index_groups=same_core, tiled=True)
    other = pairwise(mine, "lat", 1)
    first = place % 2 == 0
    next_weights = jnp.stack([jnp.where(first, mine, other), jnp.where(first, other, mine)], axis=1).reshape(HD, D)
    cell_grads = shape(CELLS, HD)
    gq, gk, gv = call(unpack_kernel, (cell_grads, cell_grads, cell_grads), grads, vmem=SMALL_BYTES)
    own = (ROWS, BLOCK, HD)
    return (gq.reshape(own), gk.reshape(own), gv.reshape(own), updated, next_weights)


def solution(mesh):
    cells = P("lat", "lon", None)
    return jax.shard_map(
        on_device,
        mesh=mesh,
        in_specs=(cells, cells, cells, cells, P(), P("lat", None), cells, cells, P("lat", "lon")),
        out_specs=(cells, cells, cells, P("lat", None), P()),
        check_vma=False,
    )
```

```python
import jax
import jax.numpy as jnp
from jax import lax
from jax.experimental import pallas as pl
from jax.experimental.pallas import tpu as pltpu
from jax.sharding import PartitionSpec as P

D = 1024
HEADS = 8
HEAD = 64
BLOCK = 64
NB = 8
ROWS = 2
HD = 512
CELLS = ROWS * BLOCK
PAIR = 2 * HEAD
HALF = BLOCK // 2
LISTS = 16
GROUP = 512

learn_rate = 0.01
decay_rate = 0.9

BF = jnp.bfloat16
F32 = jnp.float32
VMEM_BYTES = 56 * 2**20
SMALL_BYTES = 24 * 2**20
MID_BYTES = 40 * 2**20
SCALE = HEAD**-0.5


def dot(a, b, dims):
    return lax.dot_general(a, b, ((dims[:1], dims[1:]), ((), ())), preferred_element_type=F32)


def low_lanes():
    return lax.broadcasted_iota(jnp.int32, (1, PAIR), 1) < HEAD


def swap(x):
    return jnp.concatenate([x[:, HEAD:], x[:, :HEAD]], axis=1)


def fold(x):
    top, bottom = x[:HALF], x[HALF:]
    low = low_lanes()
    return jnp.where(low, top, swap(bottom)), jnp.where(low, swap(top), bottom)


def unfold(first, second):
    low = low_lanes()
    return jnp.concatenate([jnp.where(low, first, swap(second)), jnp.where(low, swap(first), second)], axis=0)


def pack_kernel(lon_ref, lat_ref, count_ref, q_ref, k_ref, v_ref, up_ref, w_ref, out_ref):
    grad = dot(up_ref[...], w_ref[...], (1, 1)).astype(BF)
    for h in range(HEADS):
        feats = slice(h * HEAD, (h + 1) * HEAD)
        kv = jnp.concatenate([k_ref[:, feats], v_ref[:, feats]], axis=1)
        qg = jnp.concatenate([q_ref[:, feats], grad[:, feats]], axis=1)
        for r in range(ROWS):
            slab = r * HEADS + h
            out_ref[slab, 0:BLOCK, :] = qg[r * BLOCK : (r + 1) * BLOCK]
            out_ref[slab, BLOCK : BLOCK + CELLS, :] = kv
    block = lax.broadcasted_iota(jnp.int32, (LISTS, PAIR), 1)
    for r in range(ROWS):
        seen = jnp.zeros((LISTS, PAIR), F32)
        for t in range(NB):
            named = jnp.where(t < count_ref[r], lon_ref[r, 0, t] * ROWS + lat_ref[r, 0, t], -1)
            seen = jnp.where(block == named, 1.0, seen)
        for h in range(HEADS):
            out_ref[r * HEADS + h, BLOCK + CELLS :, :] = seen.astype(BF)


def seen_blocks(in_ref):
    lonb = in_ref.shape[0]
    tile = (lonb, lonb * BLOCK)
    spread = lax.broadcasted_iota(jnp.int32, tile, 0) == lax.broadcasted_iota(jnp.int32, tile, 1) // BLOCK
    return dot(in_ref[:, BLOCK + CELLS, :].astype(F32), spread.astype(F32), (0, 0))[: lonb * ROWS] > 0.5


def tiles_of(in_ref):
    lonb = in_ref.shape[0]
    x = in_ref[:, 0:BLOCK, :].reshape(lonb * BLOCK, PAIR)
    return x, in_ref[:, BLOCK : BLOCK + CELLS, :].reshape(lonb * CELLS, PAIR)


def forward_kernel(in_ref, att_ref, stat_ref, score_ref):
    x, kv = tiles_of(in_ref)
    keys, cells = score_ref.shape
    k_only = jnp.where(low_lanes(), kv * jnp.asarray(SCALE, BF), jnp.zeros((), BF))
    v_t = jnp.concatenate([kv.T[HEAD:], jnp.ones((LISTS, keys), BF)], axis=0)
    seen = seen_blocks(in_ref)
    tops = []
    for g in range(0, keys, GROUP):
        scores = dot(k_only[g : g + GROUP], x, (1, 1))
        score_ref[g : g + GROUP, :] = scores
        tops += [jnp.max(scores[j : j + BLOCK], axis=0, keepdims=True) for j in range(0, GROUP, BLOCK)]
    top = jnp.max(jnp.where(seen, jnp.concatenate(tops, axis=0), -1e30), axis=0, keepdims=True)
    shift = jnp.where(seen, top, 1e30)
    att = jnp.zeros((v_t.shape[0], cells), F32)
    for g in range(0, keys, GROUP):
        probs = []
        for j in range(g, g + GROUP, BLOCK):
            prob = jnp.exp(score_ref[j : j + BLOCK, :] - shift[j // BLOCK : j // BLOCK + 1])
            probs.append(prob.astype(BF))
        att = att + dot(v_t[:, g : g + GROUP], jnp.concatenate(probs, axis=0), (1, 0))
    total = att[HEAD : HEAD + 1]
    att = (att[:HEAD] * (1.0 / total)).astype(BF)
    delta = jnp.sum(x.T[HEAD:].astype(F32) * att.astype(F32), axis=0, keepdims=True)
    row = lax.broadcasted_iota(jnp.int32, stat_ref.shape, 0)
    stat_ref[...] = jnp.where(row == 0, top + jnp.log(total), delta)
    for i in range(0, cells, PAIR):
        b = i // BLOCK
        att_ref[b], att_ref[b + 1] = fold(att[:, i : i + PAIR])


def backward_kernel(in_ref, stat_ref, out_ref):
    x, kv = tiles_of(in_ref)
    keys, cells = kv.shape[0], x.shape[0]
    low = low_lanes()
    zero = jnp.zeros((), BF)
    k_only = jnp.where(low, kv * jnp.asarray(SCALE, BF), zero)
    v_only = jnp.where(low, zero, kv)
    k_t = kv.T[:HEAD]
    shift = jnp.where(seen_blocks(in_ref), stat_ref[0:1, :], 1e30)
    delta = stat_ref[1:2, :]
    grad_q = jnp.zeros((HEAD, cells), F32)
    for g in range(0, keys, GROUP):
        scores = dot(k_only[g : g + GROUP], x, (1, 1))
        prob_grad = dot(v_only[g : g + GROUP], x, (1, 1))
        probs, score_grads = [], []
        for j in range(0, GROUP, BLOCK):
            b = (g + j) // BLOCK
            prob = jnp.exp(scores[j : j + BLOCK] - shift[b : b + 1])
            probs.append(prob.astype(BF))
            score_grads.append((prob * (prob_grad[j : j + BLOCK] - delta)).astype(BF))
        probs = jnp.concatenate(probs, axis=0)
        score_grads = jnp.concatenate(score_grads, axis=0)
        grad_q = grad_q + dot(k_t[:, g : g + GROUP], score_grads, (1, 0))
        grad_kv = jnp.where(low, dot(score_grads, x, (1, 0)) * SCALE, dot(probs, x, (1, 0)))
        out_ref[g // CELLS : (g + GROUP) // CELLS, HALF:, :] = grad_kv.astype(BF).reshape(GROUP // CELLS, CELLS, PAIR)
    grad_q = (grad_q * SCALE).astype(BF)
    for i in range(0, cells, PAIR):
        b = i // BLOCK
        out_ref[b, 0:HALF, :], out_ref[b + 1, 0:HALF, :] = fold(grad_q[:, i : i + PAIR])


def weight_kernel(place_ref, att_ref, other_att_ref, up_ref, other_up_ref, *refs):
    *out_refs, att_t = refs
    for h in range(HEADS):
        mine = unfold(att_ref[h], att_ref[HEADS + h])
        other = unfold(other_att_ref[h], other_att_ref[HEADS + h])
        for half in range(2):
            rows = slice(half * HALF, (half + 1) * HALF)
            att_t[2 * h + half] = jnp.concatenate([mine[rows], other[rows]], axis=1)
    place = place_ref[0]
    up = jnp.concatenate([up_ref[...], other_up_ref[...]], axis=0)
    for dx, out_ref in enumerate(out_refs):
        rows = jnp.concatenate([att_t[place ^ (4 * dx + 2 * dy)] for dy in range(2)], axis=0)
        out_ref[...] = dot(rows, up, (1, 0)).astype(BF).reshape(out_ref.shape)


def unpack_kernel(in_ref, gq_ref, gk_ref, gv_ref):
    gq_t = []
    for h in range(HEADS):
        feats = slice(h * HEAD, (h + 1) * HEAD)
        gq_t.append(unfold(in_ref[h, 0:HALF, :], in_ref[HEADS + h, 0:HALF, :]))
        kv = sum(in_ref[r * HEADS + h, HALF:, :].astype(F32) for r in range(ROWS)).astype(BF)
        gk_ref[:, feats] = kv[:, :HEAD]
        gv_ref[:, feats] = kv[:, HEAD:]
    gq_ref[...] = jnp.concatenate(gq_t, axis=0).T


def call(kernel, outs, *args, scratch=(), scalars=0, vmem=VMEM_BYTES):
    on_chip = [pl.BlockSpec(memory_space=pltpu.SMEM if i < scalars else pltpu.VMEM) for i in range(len(args))]
    return pl.pallas_call(
        kernel,
        out_shape=outs,
        in_specs=on_chip,
        scratch_shapes=scratch,
        compiler_params=pltpu.CompilerParams(vmem_limit_bytes=vmem),
    )(*args)


def shape(*dims, dtype=BF):
    return jax.ShapeDtypeStruct(dims, dtype)


def pairwise(x, axis, bit):
    return lax.ppermute(x, axis, [(i, i ^ bit) for i in range(lax.axis_size(axis))])


def plus(*parts):
    total = parts[0].astype(F32)
    for part in parts[1:]:
        total = total + part.astype(F32)
    return total


def joined(x, *bits):
    x = x.astype(BF)
    one, two, three = (pairwise(x, "lon", bit) for bit in bits)
    return plus(x, one) + plus(two, three)


def paired(x, bit):
    x = x.astype(BF)
    return plus(x, pairwise(x, "lon", bit))


def on_device(queries, keys, values, upstream, out_weight, average, nbr_lon, nbr_lat, counts):
    lonb = lax.axis_size("lon")
    lats = lax.axis_size("lat")
    same_core = [[c + 2 * i for i in range(lats // 2)] for c in range(2)]
    up = upstream.reshape(CELLS, D)
    other_up = pairwise(up, "lat", 1)
    slabs = call(
        pack_kernel,
        shape(lonb, BLOCK + CELLS + LISTS, PAIR),
        nbr_lon,
        nbr_lat,
        counts.reshape(ROWS),
        queries.reshape(CELLS, HD),
        keys.reshape(CELLS, HD),
        values.reshape(CELLS, HD),
        up,
        out_weight,
        scalars=3,
    )
    slabs = lax.all_to_all(slabs, "lon", 0, 0, tiled=True)
    cells = lonb * BLOCK
    att, stats = call(
        forward_kernel,
        (shape(lonb, HALF, PAIR), shape(8, cells, dtype=F32)),
        slabs,
        scratch=[pltpu.VMEM((lonb * CELLS, cells), F32)],
        vmem=MID_BYTES,
    )
    att = lax.all_to_all(att, "lon", 0, 0, tiled=True)
    grads = call(backward_kernel, shape(lonb, HALF + CELLS, PAIR), slabs, stats, vmem=MID_BYTES)
    att, grads = lax.optimization_barrier((att, grads))
    rows = HD // lats
    quarters = lats // 4
    place = lax.axis_index("lat")
    parts = call(
        weight_kernel,
        [shape(2, rows, D)] * quarters,
        place.reshape(1),
        att,
        pairwise(att, "lat", 1),
        up,
        other_up,
        scratch=[pltpu.VMEM((2 * HEADS, HALF, 2 * CELLS), BF)],
        scalars=1,
        vmem=SMALL_BYTES,
    )
    grads = lax.all_to_all(grads, "lon", 0, 0, tiled=True)
    parts = [parts[0]] + [pairwise(parts[i], "lat", 4 * i) for i in range(1, quarters)]
    near, far = (plus(*(part[i] for part in parts)).astype(BF) for i in range(2))
    both = [(i, j) for i in range(lonb) for j in range(lats)]
    across = lax.ppermute(far, ("lon", "lat"), [(i * lats + j, (i ^ 8) * lats + (j ^ 2)) for i, j in both])
    total = plus(near, pairwise(near, "lon", 8)) + plus(pairwise(far, "lat", 2), across)
    total = paired(joined(total, 1, 2, 3), 6)
    own_weight = lax.dynamic_slice_in_dim(out_weight, place * rows, rows, 0).astype(F32)
    updated = own_weight - learn_rate * total
    averaged = decay_rate * average + (1.0 - decay_rate) * updated
    averaged, grads = lax.optimization_barrier((averaged, grads))
    copies = jnp.broadcast_to(averaged.astype(BF)[None], (lats // 2, rows, D))
    mine = lax.all_to_all(copies, "lat", 0, 0, axis_index_groups=same_core, tiled=True)
    other = pairwise(mine, "lat", 1)
    first = place % 2 == 0
    next_weights = jnp.stack([jnp.where(first, mine, other), jnp.where(first, other, mine)], axis=1).reshape(HD, D)
    cell_grads = shape(CELLS, HD)
    gq, gk, gv = call(unpack_kernel, (cell_grads, cell_grads, cell_grads), grads, vmem=SMALL_BYTES)
    own = (ROWS, BLOCK, HD)
    return (gq.reshape(own), gk.reshape(own), gv.reshape(own), updated, next_weights)


def solution(mesh):
    cells = P("lat", "lon", None)
    return jax.shard_map(
        on_device,
        mesh=mesh,
        in_specs=(cells, cells, cells, cells, P(), P("lat", None), cells, cells, P("lat", "lon")),
        out_specs=(cells, cells, cells, P("lat", None), P()),
        check_vma=False,
    )
```

```python
import jax
import jax.numpy as jnp
from jax import lax
from jax.experimental import pallas as pl
from jax.experimental.pallas import tpu as pltpu
from jax.sharding import PartitionSpec as P

D = 1024
HEADS = 8
HEAD = 64
BLOCK = 64
NB = 8
ROWS = 2
HD = 512
CELLS = ROWS * BLOCK
PAIR = 2 * HEAD
HALF = BLOCK // 2
LISTS = 16
GROUP = 512

learn_rate = 0.01
decay_rate = 0.9

BF = jnp.bfloat16
F32 = jnp.float32
VMEM_BYTES = 56 * 2**20
SMALL_BYTES = 24 * 2**20
MID_BYTES = 40 * 2**20
SCALE = HEAD**-0.5


def dot(a, b, dims):
    return lax.dot_general(a, b, ((dims[:1], dims[1:]), ((), ())), preferred_element_type=F32)


def low_lanes():
    return lax.broadcasted_iota(jnp.int32, (1, PAIR), 1) < HEAD


def swap(x):
    return jnp.concatenate([x[:, HEAD:], x[:, :HEAD]], axis=1)


def fold(x):
    top, bottom = x[:HALF], x[HALF:]
    low = low_lanes()
    return jnp.where(low, top, swap(bottom)), jnp.where(low, swap(top), bottom)


def unfold(first, second):
    low = low_lanes()
    return jnp.concatenate([jnp.where(low, first, swap(second)), jnp.where(low, swap(first), second)], axis=0)


def pack_kernel(lon_ref, lat_ref, count_ref, q_ref, k_ref, v_ref, up_ref, w_ref, out_ref):
    grad = dot(up_ref[...], w_ref[...], (1, 1)).astype(BF)
    for h in range(HEADS):
        feats = slice(h * HEAD, (h + 1) * HEAD)
        kv = jnp.concatenate([k_ref[:, feats], v_ref[:, feats]], axis=1)
        qg = jnp.concatenate([q_ref[:, feats], grad[:, feats]], axis=1)
        for r in range(ROWS):
            slab = r * HEADS + h
            out_ref[slab, 0:BLOCK, :] = qg[r * BLOCK : (r + 1) * BLOCK]
            out_ref[slab, BLOCK : BLOCK + CELLS, :] = kv
    block = lax.broadcasted_iota(jnp.int32, (LISTS, PAIR), 1)
    for r in range(ROWS):
        seen = jnp.zeros((LISTS, PAIR), F32)
        for t in range(NB):
            named = jnp.where(t < count_ref[r], lon_ref[r, 0, t] * ROWS + lat_ref[r, 0, t], -1)
            seen = jnp.where(block == named, 1.0, seen)
        for h in range(HEADS):
            out_ref[r * HEADS + h, BLOCK + CELLS :, :] = seen.astype(BF)


def seen_blocks(in_ref):
    lonb = in_ref.shape[0]
    tile = (lonb, lonb * BLOCK)
    spread = lax.broadcasted_iota(jnp.int32, tile, 0) == lax.broadcasted_iota(jnp.int32, tile, 1) // BLOCK
    return dot(in_ref[:, BLOCK + CELLS, :].astype(F32), spread.astype(F32), (0, 0))[: lonb * ROWS] > 0.5


def tiles_of(in_ref):
    lonb = in_ref.shape[0]
    x = in_ref[:, 0:BLOCK, :].reshape(lonb * BLOCK, PAIR)
    return x, in_ref[:, BLOCK : BLOCK + CELLS, :].reshape(lonb * CELLS, PAIR)


def forward_kernel(in_ref, att_ref, stat_ref, score_ref):
    x, kv = tiles_of(in_ref)
    keys, cells = score_ref.shape
    k_only = jnp.where(low_lanes(), kv * jnp.asarray(SCALE, BF), jnp.zeros((), BF))
    v_t = jnp.concatenate([kv.T[HEAD:], jnp.ones((LISTS, keys), BF)], axis=0)
    seen = seen_blocks(in_ref)
    tops = []
    for g in range(0, keys, GROUP):
        scores = dot(k_only[g : g + GROUP], x, (1, 1))
        score_ref[g : g + GROUP, :] = scores
        tops += [jnp.max(scores[j : j + BLOCK], axis=0, keepdims=True) for j in range(0, GROUP, BLOCK)]
    top = jnp.max(jnp.where(seen, jnp.concatenate(tops, axis=0), -1e30), axis=0, keepdims=True)
    shift = jnp.where(seen, top, 1e30)
    att = jnp.zeros((v_t.shape[0], cells), F32)
    for g in range(0, keys, GROUP):
        probs = []
        for j in range(g, g + GROUP, BLOCK):
            prob = jnp.exp(score_ref[j : j + BLOCK, :] - shift[j // BLOCK : j // BLOCK + 1])
            probs.append(prob.astype(BF))
        att = att + dot(v_t[:, g : g + GROUP], jnp.concatenate(probs, axis=0), (1, 0))
    total = att[HEAD : HEAD + 1]
    att = (att[:HEAD] * (1.0 / total)).astype(BF)
    delta = jnp.sum(x.T[HEAD:].astype(F32) * att.astype(F32), axis=0, keepdims=True)
    row = lax.broadcasted_iota(jnp.int32, stat_ref.shape, 0)
    stat_ref[...] = jnp.where(row == 0, top + jnp.log(total), delta)
    for i in range(0, cells, PAIR):
        b = i // BLOCK
        att_ref[b], att_ref[b + 1] = fold(att[:, i : i + PAIR])


def backward_kernel(in_ref, stat_ref, out_ref):
    x, kv = tiles_of(in_ref)
    keys, cells = kv.shape[0], x.shape[0]
    low = low_lanes()
    zero = jnp.zeros((), BF)
    k_only = jnp.where(low, kv * jnp.asarray(SCALE, BF), zero)
    v_only = jnp.where(low, zero, kv)
    k_t = kv.T[:HEAD]
    shift = jnp.where(seen_blocks(in_ref), stat_ref[0:1, :], 1e30)
    delta = stat_ref[1:2, :]
    grad_q = jnp.zeros((HEAD, cells), F32)
    for g in range(0, keys, GROUP):
        scores = dot(k_only[g : g + GROUP], x, (1, 1))
        prob_grad = dot(v_only[g : g + GROUP], x, (1, 1))
        probs, score_grads = [], []
        for j in range(0, GROUP, BLOCK):
            b = (g + j) // BLOCK
            prob = jnp.exp(scores[j : j + BLOCK] - shift[b : b + 1])
            probs.append(prob.astype(BF))
            score_grads.append((prob * (prob_grad[j : j + BLOCK] - delta)).astype(BF))
        probs = jnp.concatenate(probs, axis=0)
        score_grads = jnp.concatenate(score_grads, axis=0)
        grad_q = grad_q + dot(k_t[:, g : g + GROUP], score_grads, (1, 0))
        grad_kv = jnp.where(low, dot(score_grads, x, (1, 0)) * SCALE, dot(probs, x, (1, 0)))
        out_ref[g // CELLS : (g + GROUP) // CELLS, HALF:, :] = grad_kv.astype(BF).reshape(GROUP // CELLS, CELLS, PAIR)
    grad_q = (grad_q * SCALE).astype(BF)
    for i in range(0, cells, PAIR):
        b = i // BLOCK
        out_ref[b, 0:HALF, :], out_ref[b + 1, 0:HALF, :] = fold(grad_q[:, i : i + PAIR])


def weight_kernel(place_ref, att_ref, other_att_ref, up_ref, other_up_ref, *refs):
    *out_refs, att_t = refs
    for h in range(HEADS):
        mine = unfold(att_ref[h], att_ref[HEADS + h])
        other = unfold(other_att_ref[h], other_att_ref[HEADS + h])
        for half in range(2):
            rows = slice(half * HALF, (half + 1) * HALF)
            att_t[2 * h + half] = jnp.concatenate([mine[rows], other[rows]], axis=1)
    place = place_ref[0]
    up = jnp.concatenate([up_ref[...], other_up_ref[...]], axis=0)
    for dx, out_ref in enumerate(out_refs):
        rows = jnp.concatenate([att_t[place ^ (4 * dx + 2 * dy)] for dy in range(2)], axis=0)
        out_ref[...] = dot(rows, up, (1, 0)).astype(BF).reshape(out_ref.shape)


def unpack_kernel(in_ref, gq_ref, gk_ref, gv_ref):
    gq_t = []
    for h in range(HEADS):
        feats = slice(h * HEAD, (h + 1) * HEAD)
        gq_t.append(unfold(in_ref[h, 0:HALF, :], in_ref[HEADS + h, 0:HALF, :]))
        kv = sum(in_ref[r * HEADS + h, HALF:, :].astype(F32) for r in range(ROWS)).astype(BF)
        gk_ref[:, feats] = kv[:, :HEAD]
        gv_ref[:, feats] = kv[:, HEAD:]
    gq_ref[...] = jnp.concatenate(gq_t, axis=0).T


def call(kernel, outs, *args, scratch=(), scalars=0, vmem=VMEM_BYTES):
    on_chip = [pl.BlockSpec(memory_space=pltpu.SMEM if i < scalars else pltpu.VMEM) for i in range(len(args))]
    return pl.pallas_call(
        kernel,
        out_shape=outs,
        in_specs=on_chip,
        scratch_shapes=scratch,
        compiler_params=pltpu.CompilerParams(vmem_limit_bytes=vmem),
    )(*args)


def shape(*dims, dtype=BF):
    return jax.ShapeDtypeStruct(dims, dtype)


def pairwise(x, axis, bit):
    return lax.ppermute(x, axis, [(i, i ^ bit) for i in range(lax.axis_size(axis))])


def plus(*parts):
    total = parts[0].astype(F32)
    for part in parts[1:]:
        total = total + part.astype(F32)
    return total


def joined(x, *bits):
    x = x.astype(BF)
    one, two, three = (pairwise(x, "lon", bit) for bit in bits)
    return plus(x, one) + plus(two, three)


def paired(x, bit):
    x = x.astype(BF)
    return plus(x, pairwise(x, "lon", bit))


def on_device(queries, keys, values, upstream, out_weight, average, nbr_lon, nbr_lat, counts):
    lonb = lax.axis_size("lon")
    lats = lax.axis_size("lat")
    same_core = [[c + 2 * i for i in range(lats // 2)] for c in range(2)]
    up = upstream.reshape(CELLS, D)
    other_up = pairwise(up, "lat", 1)
    slabs = call(
        pack_kernel,
        shape(lonb, BLOCK + CELLS + LISTS, PAIR),
        nbr_lon,
        nbr_lat,
        counts.reshape(ROWS),
        queries.reshape(CELLS, HD),
        keys.reshape(CELLS, HD),
        values.reshape(CELLS, HD),
        up,
        out_weight,
        scalars=3,
    )
    slabs = lax.all_to_all(slabs, "lon", 0, 0, tiled=True)
    cells = lonb * BLOCK
    att, stats = call(
        forward_kernel,
        (shape(lonb, HALF, PAIR), shape(8, cells, dtype=F32)),
        slabs,
        scratch=[pltpu.VMEM((lonb * CELLS, cells), F32)],
        vmem=MID_BYTES,
    )
    att = lax.all_to_all(att, "lon", 0, 0, tiled=True)
    grads = call(backward_kernel, shape(lonb, HALF + CELLS, PAIR), slabs, stats, vmem=MID_BYTES)
    place = lax.axis_index("lat")
    rows = HD // lats
    own_weight = lax.dynamic_slice_in_dim(out_weight, place * rows, rows, 0).astype(F32)
    kept = decay_rate * average
    att, grads, own_weight, kept = lax.optimization_barrier((att, grads, own_weight, kept))
    rows = HD // lats
    quarters = lats // 4
    place = lax.axis_index("lat")
    parts = call(
        weight_kernel,
        [shape(2, rows, D)] * quarters,
        place.reshape(1),
        att,
        pairwise(att, "lat", 1),
        up,
        other_up,
        scratch=[pltpu.VMEM((2 * HEADS, HALF, 2 * CELLS), BF)],
        scalars=1,
        vmem=SMALL_BYTES,
    )
    grads = lax.all_to_all(grads, "lon", 0, 0, tiled=True)
    parts = [parts[0]] + [pairwise(parts[i], "lat", 4 * i) for i in range(1, quarters)]
    near, far = (plus(*(part[i] for part in parts)).astype(BF) for i in range(2))
    both = [(i, j) for i in range(lonb) for j in range(lats)]
    across = lax.ppermute(far, ("lon", "lat"), [(i * lats + j, (i ^ 8) * lats + (j ^ 2)) for i, j in both])
    total = plus(near, pairwise(near, "lon", 8)) + plus(pairwise(far, "lat", 2), across)
    total = paired(joined(total, 1, 2, 3), 6)
    updated = own_weight - learn_rate * total
    averaged = kept + (1.0 - decay_rate) * updated
    averaged, grads = lax.optimization_barrier((averaged, grads))
    copies = jnp.broadcast_to(averaged.astype(BF)[None], (lats // 2, rows, D))
    mine = lax.all_to_all(copies, "lat", 0, 0, axis_index_groups=same_core, tiled=True)
    other = pairwise(mine, "lat", 1)
    first = place % 2 == 0
    next_weights = jnp.stack([jnp.where(first, mine, other), jnp.where(first, other, mine)], axis=1).reshape(HD, D)
    cell_grads = shape(CELLS, HD)
    gq, gk, gv = call(unpack_kernel, (cell_grads, cell_grads, cell_grads), grads, vmem=SMALL_BYTES)
    own = (ROWS, BLOCK, HD)
    return (gq.reshape(own), gk.reshape(own), gv.reshape(own), updated, next_weights)


def solution(mesh):
    cells = P("lat", "lon", None)
    return jax.shard_map(
        on_device,
        mesh=mesh,
        in_specs=(cells, cells, cells, cells, P(), P("lat", None), cells, cells, P("lat", "lon")),
        out_specs=(cells, cells, cells, P("lat", None), P()),
        check_vma=False,
    )
```
